512 devices in a mesh: row: 32 (over x, z), col: 16 (over y, core).
Axes of the slice: x: 4, y: 8, z: 8, core: 2. Of those that a mesh axis runs over, the one named last changes fastest.
Arguments:
- pattern: int32 [512, 16], replicated, may hold values from 0 to 511, as said below
- hamiltonian: bfloat16 [512, 16, 128, 128], P('row', 'col'), may hold values from -0.125 to 0.125
- cheb_prev: bfloat16 [512, 16, 128, 128], P('row', 'col'), may hold values from -6 to 6
- cheb_cur: bfloat16 [512, 16, 128, 128], P('row', 'col'), may hold values from -6 to 6
- kernel_in: float32 [512, 16, 128, 128], P('row', 'col'), may hold values from -6 to 6
- coefficients: float32 [2], replicated, may hold values from -1 to 1
Outputs:
- cheb_next: bfloat16 [512, 16, 128, 128], P('row', 'col')
- cheb_last: bfloat16 [512, 16, 128, 128], P('row', 'col')
- kernel: float32 [512, 16, 128, 128], P('row', 'col')
The draws below stay inside these ranges and needn't reach their ends.
Inputs may be any that keep to these rules, and one draw needn't show every extreme that they name: pattern[i, k] is congruent to k modulo 16, so the 16 entries of a row are distinct; |pattern[i, k] - i| <= 15, and in every draw some block rows i away from the ends hold the column i - (15) and some hold the column i + 15.
All inputs are finite; a program needn't handle non-finite values.
Results may differ from the reference program's by a relative error of at most 0.0065.
Values may be sent and summed in bfloat16 or wider, within the bound.
A program may use at most 128 MiB of HBM per device.

```python
import jax
import jax.numpy as jnp
from jax import lax

B = 128
K = 16
STEPS = 2
NB = 512


def draw_pattern(key, part):
    key = jax.random.fold_in(key, 11)
    jitter_key = jax.random.fold_in(key, 1)
    low_key = jax.random.fold_in(key, 2)
    high_key = jax.random.fold_in(key, 3)
    jitter = jax.random.randint(jitter_key, (NB, K), 0, K, dtype=jnp.int32)
    span = NB - 2 * K + 2
    low_row = K - 1 + jax.random.randint(low_key, (), 0, span, dtype=jnp.int32)
    step_over = 1 + jax.random.randint(high_key, (), 0, span - 1, dtype=jnp.int32)
    high_row = K - 1 + jnp.mod(low_row - (K - 1) + step_over, span)
    rows = jnp.arange(NB, dtype=jnp.int32)[:, None]
    classes = jnp.arange(K, dtype=jnp.int32)[None, :]
    low_slot = jnp.mod(low_row - (K - 1), K)
    high_slot = jnp.mod(high_row + (K - 1), K)
    jitter = jnp.where((rows == low_row) & (classes == low_slot), jnp.zeros((), jnp.int32), jitter)
    jitter = jnp.where((rows == high_row) & (classes == high_slot), jnp.full((), K - 1, jnp.int32), jitter)
    begin = rows - (K - 1) + jitter
    column = begin + jnp.mod(classes - begin, K)
    column = jnp.where(column < 0, column + K, column)
    column = jnp.where(column >= NB, column - K, column)
    return column.astype(jnp.int32)


def shard_levels(own_key, shape, split, low, largest):
    def one(axis_at, shards_of):
        heights = jax.random.uniform(jax.random.fold_in(jax.random.fold_in(own_key, 6), axis_at), (shards_of,), jnp.float32, low / len(split), largest / len(split))
        return jnp.repeat(jnp.exp(heights), shape[axis_at] // shards_of).reshape((-1,) + (1,) * (len(shape) - axis_at - 1))

    gain = one(*split[0])
    for cut in split[1:]:
        gain = gain * one(*cut)
    return gain


def centred(key, extent, spread, limit, cuts=(), held_as=jnp.bfloat16):
    array = jax.random.normal(key, extent, jnp.float32) * spread
    if len(cuts) > 0:
        array = shard_levels(key, extent, cuts, -0.22, 0.18) * array
    return jnp.clip(array, min=-limit, max=limit).astype(held_as)


def setup_inputs(seed: int = 0) -> dict:
    keys = jax.random.split(jax.random.key(seed), 7)
    pattern = draw_pattern(jax.random.fold_in(keys[6], 71), 0)
    hamiltonian = centred(keys[1], (NB, K, B, B), (K * B) ** -0.5, 0.125, ((0, 32), (1, 16)))
    cheb_prev = centred(keys[2], (NB, K, B, B), 1.0, 6.0, ((0, 32), (1, 16)))
    cheb_cur = centred(keys[3], (NB, K, B, B), 1.0, 6.0, ((0, 32), (1, 16)))
    kernel_in = centred(keys[4], (NB, K, B, B), 1.0, 6.0, ((0, 32), (1, 16)), jnp.float32)
    coefficients = jnp.clip(jax.random.uniform(keys[5], (STEPS,), jnp.float32, -1.0, 1.0), -1.0, 1.0)
    return {"pattern": pattern, "hamiltonian": hamiltonian, "cheb_prev": cheb_prev, "cheb_cur": cheb_cur, "kernel_in": kernel_in, "coefficients": coefficients}


def advance(pattern, hamiltonian, current):
    def one_row(index):
        targets = pattern[index]
        picked = current[targets]
        matches = pattern[targets] == pattern[index][None, :]
        picked = jnp.where(matches[:, :, None, None], picked, jnp.zeros((), current.dtype))
        return jnp.einsum("jab,jkbc->kac", hamiltonian[index].astype(jnp.float32), picked.astype(jnp.float32))

    return lax.map(one_row, jnp.arange(pattern.shape[0], dtype=jnp.int32))


def reference(pattern, hamiltonian, cheb_prev, cheb_cur, kernel_in, coefficients):
    previous = cheb_prev
    current = cheb_cur
    kernel = kernel_in
    for index in range(STEPS):
        product = advance(pattern, hamiltonian, current)
        fresh = (2.0 * product - previous.astype(jnp.float32)).astype(jnp.bfloat16)
        kernel = kernel + coefficients[index] * fresh.astype(jnp.float32)
        previous, current = current, fresh
    return current, previous, kernel
```

```python
import functools

import jax
import jax.numpy as jnp
from jax import lax
from jax.experimental import pallas as pl
from jax.experimental.pallas import tpu as pltpu
from jax.sharding import PartitionSpec as P

STEPS = 2
PHASES = 4
SUBS = 2
AHEAD = 2
MESH = pl.DeviceIdType.MESH


def hop_order(reach, even):
    both = []
    for way in range(2):
        first, second = (0, 1) if way == 0 else (1, 0)
        order = []
        for hop in range(1, reach + 1):
            order.append((hop, first))
            if hop < reach or not even:
                order.append((hop, second))
        both.append(order)
    return both


def kernel(
    chips,
    pattern,
    coefficients,
    ham,
    prev,
    cur,
    kin,
    next_out,
    last_out,
    kernel_out,
    held,
    near,
    near2,
    before,
    total,
    newest,
    picks,
    ring_send,
    ring_recv,
    pair_send,
    pair_recv,
    own_send,
    own_recv,
    halo_send,
    halo_recv,
    halo2_send,
    halo2_recv,
    local,
):
    classes, rows = held.shape[0], held.shape[1]
    band = rows // PHASES
    part = band // SUBS
    reach = chips // 2
    orders = hop_order(reach, chips % 2 == 0)
    items = len(orders[0])

    row_count = lax.axis_size("row")
    me_row, me_col = lax.axis_index("row"), lax.axis_index("col")
    chip, core = me_col // 2, me_col % 2
    start = me_row * rows
    sibling = (me_row, chip * 2 + (1 - core))
    ring = (
        (me_row, ((chip + 1) % chips) * 2 + core),
        (me_row, ((chip + chips - 1) % chips) * 2 + core),
    )
    above = ((me_row + row_count - 1) % row_count, me_col)
    below = ((me_row + 1) % row_count, me_col)

    barrier = pltpu.get_barrier_semaphore()
    for other in (*ring, sibling, above, below):
        pl.semaphore_signal(barrier, inc=1, device_id=other, device_id_type=MESH)
    pl.semaphore_wait(barrier, 5)

    def owner(way, hop, side):
        step = chips - hop if way == 0 else hop
        return ((chip + step) % chips) * 2 + side

    def span(phase, half):
        return pl.ds(phase * band + half * part, part)

    def ring_copy(way, phase, n):
        hop, half = orders[way][n]
        where = span(phase, half)
        if hop == 1:
            src, dst = ham.at[where], held.at[me_col, where]
        else:
            src = dst = held.at[owner(way, hop - 1, core), where]
        return pltpu.make_async_remote_copy(
            src_ref=src,
            dst_ref=dst,
            send_sem=ring_send.at[way, phase, n],
            recv_sem=ring_recv.at[way, phase, n],
            device_id=ring[way],
            device_id_type=MESH,
        )

    def ring_arrival(way, phase, n):
        hop, half = orders[way][n]
        piece = held.at[owner(way, hop, core), span(phase, half)]
        return pltpu.make_async_remote_copy(
            src_ref=piece,
            dst_ref=piece,
            send_sem=ring_send.at[way, phase, n],
            recv_sem=ring_recv.at[way, phase, n],
            device_id=ring[way],
            device_id_type=MESH,
        )

    def pair_copy(way, phase, n, side):
        hop, half = orders[way][n]
        piece = held.at[owner(way, hop, side), span(phase, half)]
        return pltpu.make_async_remote_copy(
            src_ref=piece,
            dst_ref=piece,
            send_sem=pair_send.at[way, phase, n],
            recv_sem=pair_recv.at[way, phase, n],
            device_id=sibling,
            device_id_type=MESH,
        )

    def own_copy(phase):
        where = pl.ds(phase * band, band)
        return pltpu.make_async_remote_copy(
            src_ref=ham.at[where],
            dst_ref=held.at[me_col, where],
            send_sem=own_send.at[phase],
            recv_sem=own_recv.at[phase],
            device_id=sibling,
            device_id_type=MESH,
        )

    def halo_copy(side):
        place = pl.ds(0, rows) if side == 0 else pl.ds(2 * rows, rows)
        return pltpu.make_async_remote_copy(
            src_ref=cur,
            dst_ref=near.at[place],
            send_sem=halo_send.at[side],
            recv_sem=halo_recv.at[side],
            device_id=below if side == 0 else above,
            device_id_type=MESH,
        )

    def halo2_copy(side, phase):
        offset = 0 if side == 0 else 2 * rows
        return pltpu.make_async_remote_copy(
            src_ref=near2.at[pl.ds(rows + phase * band, band)],
            dst_ref=near2.at[pl.ds(offset + phase * band, band)],
            send_sem=halo2_send.at[side, phase],
            recv_sem=halo2_recv.at[side, phase],
            device_id=below if side == 0 else above,
            device_id_type=MESH,
        )

    for n in range(AHEAD):
        for way in range(2):
            ring_copy(way, 0, n).start()
    for side in range(2):
        halo_copy(side).start()
    loads = (
        pltpu.make_async_copy(ham, held.at[me_col], local.at[0]),
        pltpu.make_async_copy(cur, near.at[pl.ds(rows, rows)], local.at[1]),
        pltpu.make_async_copy(prev, before, local.at[2]),
        pltpu.make_async_copy(kin, total, local.at[3]),
    )
    for load in loads:
        load.start()
    for phase in range(PHASES):
        own_copy(phase).start()

    near[3 * rows] = jnp.zeros(near.shape[1:], near.dtype)
    near2[3 * rows] = jnp.zeros(near2.shape[1:], near2.dtype)

    def choose(i, carry):
        wanted = pattern[me_col, start + i]
        for j in range(classes):
            column = pattern[j, start + i]
            match = pattern[me_col, column] == wanted
            place = jnp.clip(column - start + rows, 0, 3 * rows - 1)
            picks[i, j] = jnp.where(match, place, 3 * rows)
        return carry

    lax.fori_loop(0, rows, choose, 0)

    def product(source, i):
        acc = None
        for j in range(0, classes, 2):
            left = jnp.concatenate([held[j, i], held[j + 1, i]], axis=1)
            right = jnp.concatenate([source[picks[i, j]], source[picks[i, j + 1]]], axis=0)
            term = jnp.dot(left, right, preferred_element_type=jnp.float32)
            acc = term if acc is None else acc + term
        return acc

    def first_step(i):
        fresh = (2.0 * product(near, i) - before[i].astype(jnp.float32)).astype(jnp.bfloat16)
        near2[rows + i] = fresh
        total[i] = total[i] + coefficients[0] * fresh.astype(jnp.float32)

    def phase_ready(phase):
        own_copy(phase).wait_recv()
        for n in range(items):
            for way in range(2):
                pair_copy(way, phase, n, 1 - core).wait_recv()

    def step_ready():
        for load in loads:
            load.wait()
        for side in range(2):
            halo_copy(side).wait_recv()

    def run_phase(phase, carry):
        for n in range(items):
            for way in range(2):
                ring_arrival(way, phase, n).wait_recv()
                pair_copy(way, phase, n, core).start()
                later = n + AHEAD
                if later < items:
                    ring_copy(way, phase, later).start()
                else:

                    @pl.when(phase + 1 < PHASES)
                    def _():
                        ring_copy(way, phase + 1, later - items).start()

            if n == 1:

                @pl.when(phase == 1)
                def _():
                    step_ready()

            if 1 <= n <= band:

                @pl.when(phase > 0)
                def _():
                    if n == 1:
                        phase_ready(phase - 1)
                    first_step((phase - 1) * band + n - 1)
                    if n == band:
                        for side in range(2):
                            halo2_copy(side, phase - 1).start()

        return carry

    lax.fori_loop(0, PHASES, run_phase, 0)
    phase_ready(PHASES - 1)

    def rest(i, carry):
        first_step(i)
        return carry

    lax.fori_loop((PHASES - 1) * band, rows, rest, 0)
    for side in range(2):
        halo2_copy(side, PHASES - 1).start()
    save_last = pltpu.make_async_copy(near2.at[pl.ds(rows, rows)], last_out, local.at[4])
    save_last.start()
    for phase in range(PHASES):
        for side in range(2):
            halo2_copy(side, phase).wait_recv()

    def second_step(i, carry):
        fresh = (2.0 * product(near2, i) - near[rows + i].astype(jnp.float32)).astype(jnp.bfloat16)
        newest[i] = fresh
        total[i] = total[i] + coefficients[1] * fresh.astype(jnp.float32)
        return carry

    lax.fori_loop(0, rows, second_step, 0)
    saves = (
        pltpu.make_async_copy(newest, next_out, local.at[5]),
        pltpu.make_async_copy(total, kernel_out, local.at[6]),
    )
    for save in saves:
        save.start()

    def drain(phase, carry):
        own_copy(phase).wait_send()
        for side in range(2):
            halo2_copy(side, phase).wait_send()
        for n in range(items):
            for way in range(2):
                ring_copy(way, phase, n).wait_send()
                pair_copy(way, phase, n, core).wait_send()
        return carry

    lax.fori_loop(0, PHASES, drain, 0)
    for side in range(2):
        halo_copy(side).wait_send()
    save_last.wait()
    for save in saves:
        save.wait()


def shards(chips, pattern, hamiltonian, cheb_prev, cheb_cur, kernel_in, coefficients):
    rows, _, b, _ = hamiltonian.shape
    classes = pattern.shape[1]
    items = len(hop_order(chips // 2, chips % 2 == 0)[0])
    blocks = (rows, b, b)
    dma = pltpu.SemaphoreType.DMA
    any_spec = pl.BlockSpec(memory_space=pl.ANY)
    smem_spec = pl.BlockSpec(memory_space=pltpu.SMEM)
    outs = pl.pallas_call(
        functools.partial(kernel, chips),
        out_shape=(
            jax.ShapeDtypeStruct(blocks, jnp.bfloat16),
            jax.ShapeDtypeStruct(blocks, jnp.bfloat16),
            jax.ShapeDtypeStruct(blocks, jnp.float32),
        ),
        in_specs=[smem_spec, smem_spec] + [any_spec] * 4,
        out_specs=(any_spec,) * 3,
        scratch_shapes=[
            pltpu.VMEM((classes, rows, b, b), jnp.bfloat16),
            pltpu.VMEM((3 * rows + 1, b, b), jnp.bfloat16),
            pltpu.VMEM((3 * rows + 1, b, b), jnp.bfloat16),
            pltpu.VMEM(blocks, jnp.bfloat16),
            pltpu.VMEM(blocks, jnp.float32),
            pltpu.VMEM(blocks, jnp.bfloat16),
            pltpu.SMEM((rows, classes), jnp.int32),
            dma((2, PHASES, items)),
            dma((2, PHASES, items)),
            dma((2, PHASES, items)),
            dma((2, PHASES, items)),
            dma((PHASES,)),
            dma((PHASES,)),
            dma((2,)),
            dma((2,)),
            dma((2, PHASES)),
            dma((2, PHASES)),
            dma((7,)),
        ],
        compiler_params=pltpu.CompilerParams(
            collective_id=0, has_side_effects=True, vmem_limit_bytes=60 * 2**20
        ),
    )(
        pattern.T,
        coefficients,
        hamiltonian.reshape(blocks),
        cheb_prev.reshape(blocks),
        cheb_cur.reshape(blocks),
        kernel_in.reshape(blocks),
    )
    return tuple(x.reshape(rows, 1, b, b) for x in outs)


def solution(mesh):
    return jax.shard_map(
        functools.partial(shards, mesh.shape["col"] // 2),
        mesh=mesh,
        in_specs=(P(), *[P("row", "col", None, None)] * 4, P()),
        out_specs=(P("row", "col", None, None),) * 3,
        check_vma=False,
    )
```
